32 devices in a mesh: dom: 2 (over core), fsdp: 16 (over z, y, x).
Axes of the slice: x: 2, y: 2, z: 4, core: 2. Of those that a mesh axis runs over, the one named last changes fastest.
Arguments:
- weights: bfloat16 [2, 16, 640, 3584], P('dom', 'fsdp'), may hold values from -6 to 6
- activations: bfloat16 [2, 2, 320, 2560], P('dom', None, 'fsdp'), may hold values from -6 to 6
- cotangents: bfloat16 [2, 2, 320, 14336], P('dom', None, 'fsdp'), may hold values from -0.3125 to 0.3125
- lengths: int32 [2, 2, 16], P('dom', None, 'fsdp'), may hold values from 1 to 20, 240 in all within a row
Outputs:
- merged: bfloat16 [16, 640, 3584], P('fsdp')
The draws below stay inside these ranges and needn't reach their ends.
Inputs may be any that keep to these rules, and one draw needn't show every extreme that they name: In every domain and micro-batch the lengths sum to 240, and some block is full.
All inputs are finite; a program needn't handle non-finite values.
Results may differ from the reference program's by a relative error of at most 0.018.
Values may be sent and summed in bfloat16 or wider, within the bound.
A program may use at most 64 MiB of HBM per device.

```python
import math
import jax
import jax.numpy as jnp
import numpy as np
from jax import lax

D = 2560
F = 14336
MB = 2
RB = 4
SLOTS = 20
CB = 4
TR = 640
TC = 3584
TILES = 16
DOMAINS = 2
TOKENS = 320
N_FSDP = 16


def steps_of(own_key, dims, cuts, smallest, largest):
    def one(axis_at, blocks):
        steps = jax.random.uniform(jax.random.fold_in(jax.random.fold_in(own_key, 6), axis_at), (blocks,), jnp.float32, smallest / len(cuts), largest / len(cuts))
        return jnp.repeat(jnp.exp(steps), dims[axis_at] // blocks).reshape((-1,) + (1,) * (len(dims) - axis_at - 1))

    level = one(*cuts[0])
    for cut in cuts[1:]:
        level = level * one(*cut)
    return level


def split_up(count, total, most, skew):
    weights = [(1 << 20) // math.isqrt(grade ** skew) + 1 for grade in range(2, count + 1)]
    surplus, holding = total - most - (count - 1), [1] * (count - 1)
    while surplus > 0:
        candidates = [i for i in range(count - 1) if holding[i] < most]
        whole, remaining = sum([weights[i] for i in candidates]), surplus
        for i in candidates:
            extra = min(most - holding[i], max(1, remaining * weights[i] // whole), surplus)
            holding[i] = holding[i] + extra
            surplus = surplus - extra
    return np.array([most] + holding)


def ragged(rng, count, total, reach, lean):
    if count == 2:
        one = jax.random.randint(rng, (), max(1, total - reach), min(reach, total - 1) + 1)
        return jnp.stack([one, total - one])
    tallies = jnp.asarray(split_up(count, total, reach, lean), jnp.int32)
    pairs = (count - 1) // 2
    giver, taker = tallies[1:1 + 2 * pairs:2], tallies[2:2 + 2 * pairs:2]
    slack = jnp.minimum(giver - 1, reach - taker)
    moved = jax.random.randint(jax.random.fold_in(rng, 1), (pairs,), 0, 1 << 20) % (slack + 1)
    tallies = tallies.at[1:1 + 2 * pairs:2].set(giver - moved).at[2:2 + 2 * pairs:2].set(taker + moved)
    return tallies[jax.random.permutation(jax.random.fold_in(rng, 2), count)]


def centred(own_key, extent, scale, limit, split=(), kind=jnp.bfloat16):
    drawn = jax.random.normal(own_key, extent, jnp.float32) * scale
    if len(split) > 0:
        drawn = steps_of(own_key, extent, split, -0.22, 0.18) * drawn
    return jnp.clip(drawn, min=-limit, max=limit).astype(kind)


def setup_inputs(seed: int = 0) -> dict:
    splits = jax.random.split(jax.random.key(seed), 5)
    weights = centred(splits[0], (DOMAINS, TILES, TR, TC), 1.0, 6.0, ((0, 2), (1, 16)))
    activations = centred(splits[1], (DOMAINS, MB, TOKENS, D), 1.0, 6.0, ((0, 2), (2, 16)))
    cotangents = centred(splits[2], (DOMAINS, MB, TOKENS, F), TOKENS ** -0.5, 0.3125, ((0, 2), (2, 16)))
    lengths = jax.vmap(lambda own: ragged(own, N_FSDP, 3 * SLOTS * N_FSDP // 4, SLOTS, 2))(jax.random.split(splits[3], DOMAINS * MB)).reshape((DOMAINS, MB, N_FSDP)).astype(jnp.int32)
    return dict(weights=weights, activations=activations, cotangents=cotangents, lengths=lengths)


damping = 0.001


def domain_terms(weight, feats, cots, lens):
    pos = jnp.arange(TOKENS) % SLOTS
    owner = jnp.arange(TOKENS) // SLOTS
    fisher = jnp.zeros((D, F), jnp.float32)
    for step in range(MB):
        mask = (pos < lens[step][owner]).astype(jnp.bfloat16)
        masked = feats[step] * mask[:, None]
        grad = jnp.dot(masked.T, cots[step], preferred_element_type=jnp.float32)
        fisher = fisher + grad * grad
    fisher = fisher / MB
    tiled = fisher.reshape(RB, TR, CB, TC).transpose(0, 2, 1, 3).reshape(TILES, TR, TC)
    term = tiled + damping
    numer_term = (term * weight.astype(jnp.float32)).astype(jnp.bfloat16)
    denom_term = term.astype(jnp.bfloat16)
    return numer_term, denom_term


def reference(weights, activations, cotangents, lengths):
    def accumulate(carry, idx):
        numer_term, denom_term = domain_terms(weights[idx], activations[idx], cotangents[idx], lengths[idx])
        return (carry[0] + numer_term.astype(jnp.float32), carry[1] + denom_term.astype(jnp.float32)), None

    start = (jnp.zeros((TILES, TR, TC), jnp.float32), jnp.zeros((TILES, TR, TC), jnp.float32))
    (numer, denom), unused = lax.scan(accumulate, start, jnp.arange(DOMAINS))
    return (numer / denom).astype(jnp.bfloat16)
```

```python
import functools

import jax
import jax.numpy as jnp
from jax import lax
from jax.experimental import pallas as pl
from jax.experimental.pallas import tpu as pltpu
from jax.sharding import PartitionSpec as P

damping = 0.001
MESH = pl.DeviceIdType.MESH


def kernel(doms, row_blocks, col_blocks, feats, cots, weights, out, held, numer, denom, numer_in, denom_in,
           up_sem, down_sem, recv_sem, term_send, term_recv, out_send, out_recv):
    dom = lax.axis_index("dom")
    me = lax.axis_index("fsdp")
    row = lax.div(me, col_blocks)
    chunks, _, tokens, width = held.shape
    batches, rows, depth = feats.shape
    share = rows // doms
    tile = 128 if rows % 128 == 0 else rows
    piece = 64 if share % 64 == 0 else share
    last = row_blocks - 1

    barrier = pltpu.get_barrier_semaphore()
    for step in range(1, row_blocks):
        other = lax.rem(me + step * col_blocks, row_blocks * col_blocks)
        pl.semaphore_signal(barrier, inc=1, device_id=(dom, other), device_id_type=MESH)
    for step in range(1, doms):
        pl.semaphore_signal(barrier, inc=1, device_id=(lax.rem(dom + step, doms), me), device_id_type=MESH)
    pl.semaphore_wait(barrier, row_blocks - 1 + doms - 1)

    def hop(chunk, source, sem, way):
        return pltpu.make_async_remote_copy(
            src_ref=held.at[chunk, source],
            dst_ref=held.at[chunk, source],
            send_sem=sem.at[chunk, source],
            recv_sem=recv_sem.at[chunk, source],
            device_id=(dom, me + way * col_blocks),
            device_id_type=MESH,
        )

    def term_copy(chunk, peer_step, which):
        src, dst = ((numer, numer_in), (denom, denom_in))[which]
        peer = lax.rem(dom + peer_step, doms)
        return pltpu.make_async_remote_copy(
            src_ref=src.at[chunk, pl.ds(pl.multiple_of(peer * share, share), share)],
            dst_ref=dst.at[chunk, doms - 1 - peer_step],
            send_sem=term_send.at[chunk, peer_step - 1, which],
            recv_sem=term_recv.at[chunk, doms - 1 - peer_step, which],
            device_id=(peer, me),
            device_id_type=MESH,
        )

    def term_arrival(chunk, slot, which):
        dst = (numer_in, denom_in)[which]
        return pltpu.make_async_copy(dst.at[chunk, slot], dst.at[chunk, slot], term_recv.at[chunk, slot, which])

    def out_copy(chunk, peer_step):
        where = out.at[
            pl.ds(pl.multiple_of(dom * share, share), share), pl.ds(pl.multiple_of(chunk * width, width), width)
        ]
        return pltpu.make_async_remote_copy(
            src_ref=where,
            dst_ref=where,
            send_sem=out_send.at[chunk, peer_step - 1],
            recv_sem=out_recv.at[chunk, doms - 1 - peer_step],
            device_id=(lax.rem(dom + peer_step, doms), me),
            device_id_type=MESH,
        )

    def out_arrival(chunk, slot):
        peer = lax.rem(dom + slot + 1, doms)
        where = out.at[
            pl.ds(pl.multiple_of(peer * share, share), share), pl.ds(pl.multiple_of(chunk * width, width), width)
        ]
        return pltpu.make_async_copy(where, where, out_recv.at[chunk, slot])

    def compute(chunk):
        columns = pl.ds(pl.multiple_of(chunk * width, width), width)

        @pl.loop(0, rows // tile)
        def _(at):
            here = pl.ds(pl.multiple_of(at * tile, tile), tile)
            right = held[chunk].reshape(depth, width)
            total = None
            for batch in range(batches):
                grad = jnp.dot(feats[batch, here], right, preferred_element_type=jnp.float32)
                total = grad * grad if total is None else total + grad * grad
            term = total / batches + damping
            denom[chunk, here] = term.astype(jnp.bfloat16)
            numer[chunk, here] = (term * weights[here, columns].astype(jnp.float32)).astype(jnp.bfloat16)

    def merge(chunk):
        columns = pl.ds(pl.multiple_of(chunk * width, width), width)

        @pl.loop(0, share // piece)
        def _(at):
            mine = pl.ds(pl.multiple_of(dom * share + at * piece, piece), piece)
            there = pl.ds(pl.multiple_of(at * piece, piece), piece)
            top = numer[chunk, mine].astype(jnp.float32)
            low = denom[chunk, mine].astype(jnp.float32)
            for slot in range(doms - 1):
                top = top + numer_in[chunk, slot, there].astype(jnp.float32)
                low = low + denom_in[chunk, slot, there].astype(jnp.float32)
            out[mine, columns] = (top / low).astype(jnp.bfloat16)

    def inside(chunk):
        return jnp.logical_and(chunk >= 0, chunk < chunks)

    @pl.loop(0, chunks + row_blocks)
    def _(step):
        @pl.when(step < chunks)
        def _():
            held[step, row] = cots[step]

            @pl.when(row < last)
            def _():
                hop(step, row, up_sem, 1).start()

            @pl.when(row > 0)
            def _():
                hop(step, row, down_sem, -1).start()

        for far in range(1, row_blocks):
            chunk = step - far

            @pl.when(jnp.logical_and(inside(chunk), row - far >= 0))
            def _():
                hop(chunk, row - far, up_sem, 1).wait_recv()

                @pl.when(row < last)
                def _():
                    hop(chunk, row - far, up_sem, 1).start()

            @pl.when(jnp.logical_and(inside(chunk), row + far <= last))
            def _():
                hop(chunk, row + far, down_sem, -1).wait_recv()

                @pl.when(row > 0)
                def _():
                    hop(chunk, row + far, down_sem, -1).start()

        ready = step - last

        @pl.when(inside(ready))
        def _():
            compute(ready)
            for peer_step in range(1, doms):
                for which in range(2):
                    term_copy(ready, peer_step, which).start()

        before = ready - 1

        @pl.when(inside(before))
        def _():
            for slot in range(doms - 1):
                for which in range(2):
                    term_arrival(before, slot, which).wait()
            merge(before)
            for peer_step in range(1, doms):
                out_copy(before, peer_step).start()

    @pl.loop(0, chunks)
    def _(chunk):
        for source in range(row_blocks):
            @pl.when(jnp.logical_and(row < last, source <= row))
            def _():
                hop(chunk, source, up_sem, 1).wait_send()

            @pl.when(jnp.logical_and(row > 0, source >= row))
            def _():
                hop(chunk, source, down_sem, -1).wait_send()

        for peer_step in range(1, doms):
            for which in range(2):
                term_copy(chunk, peer_step, which).wait_send()
            out_copy(chunk, peer_step).wait_send()
        for slot in range(doms - 1):
            out_arrival(chunk, slot).wait()


def chunk_width(cols):
    for width in (512, 384, 256, 128):
        if cols % width == 0:
            return width
    return cols


def body(weights, activations, cotangents, lengths):
    devices = lax.axis_size("fsdp")
    doms = lax.axis_size("dom")
    rows, cols = weights.shape[2:]
    batches, slots = activations.shape[1:3]
    row_blocks = activations.shape[3] // rows
    col_blocks = devices // row_blocks
    across = [[r * col_blocks + c for c in range(col_blocks)] for r in range(row_blocks)]
    along = [[r * col_blocks + c for r in range(row_blocks)] for c in range(col_blocks)]
    width = chunk_width(cols)
    chunks = cols // width
    tokens = col_blocks * batches * slots
    depth = row_blocks * tokens

    mask = (jnp.arange(slots)[None, :] < lengths[0, :, 0:1]).astype(jnp.bfloat16)
    feats = activations[0] * mask[:, :, None]
    feats = feats.reshape(batches * slots, row_blocks, rows).transpose(1, 0, 2)
    feats = lax.all_to_all(feats, "fsdp", 0, 0, axis_index_groups=along, tiled=True)
    feats = lax.all_gather(feats, "fsdp", axis_index_groups=across)
    feats = feats.reshape(col_blocks, row_blocks, batches, slots, rows).transpose(4, 1, 0, 2, 3)
    own = jnp.arange(batches)[:, None] == jnp.arange(batches)[None, :]
    feats = jnp.where(own[:, None, None, None, :, None], feats[None], 0).reshape(batches, rows, depth)

    cots = cotangents[0].reshape(batches * slots, col_blocks, chunks, width).transpose(1, 2, 0, 3)
    cots = lax.all_to_all(cots, "fsdp", 0, 0, axis_index_groups=across, tiled=True)
    cots = cots.transpose(1, 0, 2, 3).reshape(chunks, tokens, width)

    share = rows // doms
    vmem = pl.BlockSpec(memory_space=pltpu.VMEM)
    bf16 = jnp.bfloat16
    merged = pl.pallas_call(
        functools.partial(kernel, doms, row_blocks, col_blocks),
        out_shape=jax.ShapeDtypeStruct((rows, cols), bf16),
        in_specs=[vmem] * 3,
        out_specs=vmem,
        scratch_shapes=[
            pltpu.VMEM((chunks, row_blocks, tokens, width), bf16),
            pltpu.VMEM((chunks, rows, width), bf16),
            pltpu.VMEM((chunks, rows, width), bf16),
            pltpu.VMEM((chunks, doms - 1, share, width), bf16),
            pltpu.VMEM((chunks, doms - 1, share, width), bf16),
            pltpu.SemaphoreType.DMA((chunks, row_blocks)),
            pltpu.SemaphoreType.DMA((chunks, row_blocks)),
            pltpu.SemaphoreType.DMA((chunks, row_blocks)),
            pltpu.SemaphoreType.DMA((chunks, doms - 1, 2)),
            pltpu.SemaphoreType.DMA((chunks, doms - 1, 2)),
            pltpu.SemaphoreType.DMA((chunks, doms - 1)),
            pltpu.SemaphoreType.DMA((chunks, doms - 1)),
        ],
        compiler_params=pltpu.CompilerParams(
            collective_id=0, has_side_effects=True, vmem_limit_bytes=56 << 20
        ),
    )(feats, cots, weights[0, 0])
    return merged[None]


def solution(mesh):
    return jax.shard_map(
        body,
        mesh=mesh,
        in_specs=(
            P("dom", "fsdp", None, None),
            P("dom", None, "fsdp", None),
            P("dom", None, "fsdp", None),
            P("dom", None, "fsdp"),
        ),
        out_specs=P("fsdp", None, None),
        check_vma=False,
    )
```

```python
import functools

import jax
import jax.numpy as jnp
from jax import lax
from jax.experimental import pallas as pl
from jax.experimental.pallas import tpu as pltpu
from jax.sharding import PartitionSpec as P

damping = 0.001
MESH = pl.DeviceIdType.MESH


def kernel(doms, row_blocks, col_blocks, live, feats, cots, weights, out, feat_box, feat_all, feat_rows, feat_cols,
           inbox, held, numer, denom, numer_in, denom_in, along_send, along_recv, across_send, across_recv,
           piece_send, piece_recv, up_sem, down_sem, recv_sem, term_send, term_recv, out_send, out_recv):
    dom = lax.axis_index("dom")
    me = lax.axis_index("fsdp")
    row = lax.div(me, col_blocks)
    col = lax.rem(me, col_blocks)
    chunks, _, tokens, width = held.shape
    batches, rows, depth = feat_cols.shape
    share = rows // doms
    tile = 128 if rows % 128 == 0 else rows
    piece = 64 if share % 64 == 0 else share
    strip = 128 if depth % 128 == 0 else depth
    last = row_blocks - 1

    barrier = pltpu.get_barrier_semaphore()
    for step in range(1, row_blocks):
        other = lax.rem(me + step * col_blocks, row_blocks * col_blocks)
        pl.semaphore_signal(barrier, inc=1, device_id=(dom, other), device_id_type=MESH)
    for step in range(1, col_blocks):
        other = row * col_blocks + lax.rem(col + step, col_blocks)
        pl.semaphore_signal(barrier, inc=1, device_id=(dom, other), device_id_type=MESH)
    for step in range(1, doms):
        pl.semaphore_signal(barrier, inc=1, device_id=(lax.rem(dom + step, doms), me), device_id_type=MESH)
    pl.semaphore_wait(barrier, row_blocks - 1 + col_blocks - 1 + doms - 1)

    def feat_along(step):
        peer = lax.rem(row + step, row_blocks)
        return pltpu.make_async_remote_copy(
            src_ref=feats.at[peer],
            dst_ref=feat_box.at[row],
            send_sem=along_send.at[step - 1],
            recv_sem=along_recv.at[row_blocks - 1 - step],
            device_id=(dom, peer * col_blocks + col),
            device_id_type=MESH,
        )

    def feat_along_arrival(slot):
        dst = feat_box.at[lax.rem(row + slot + 1, row_blocks)]
        return pltpu.make_async_copy(dst, dst, along_recv.at[slot])

    def feat_across(step):
        return pltpu.make_async_remote_copy(
            src_ref=feat_box,
            dst_ref=feat_all.at[col_blocks - 1 - step],
            send_sem=across_send.at[step - 1],
            recv_sem=across_recv.at[col_blocks - 1 - step],
            device_id=(dom, row * col_blocks + lax.rem(col + step, col_blocks)),
            device_id_type=MESH,
        )

    def feat_across_arrival(slot):
        dst = feat_all.at[slot]
        return pltpu.make_async_copy(dst, dst, across_recv.at[slot])

    def piece_copy(chunk, step):
        peer = lax.rem(col + step, col_blocks)
        return pltpu.make_async_remote_copy(
            src_ref=cots.at[peer, chunk],
            dst_ref=inbox.at[chunk, col_blocks - 1 - step],
            send_sem=piece_send.at[chunk, step - 1],
            recv_sem=piece_recv.at[chunk, col_blocks - 1 - step],
            device_id=(dom, row * col_blocks + peer),
            device_id_type=MESH,
        )

    def piece_arrival(chunk, slot):
        dst = inbox.at[chunk, slot]
        return pltpu.make_async_copy(dst, dst, piece_recv.at[chunk, slot])

    def join(parts):
        return jnp.concatenate([part.astype(jnp.float32)[:live] for part in parts], axis=0)

    def assemble(chunk):
        parts = [cots[col, chunk]] + [inbox[chunk, slot] for slot in range(col_blocks - 1)]
        held[chunk, row] = join(parts).astype(jnp.bfloat16)

    def turn_feats():
        @pl.loop(0, row_blocks)
        def _(at):
            parts = [feat_box[at]] + [feat_all[slot, at] for slot in range(col_blocks - 1)]
            feat_rows[pl.ds(pl.multiple_of(at * tokens, tokens), tokens)] = join(parts)

        @pl.loop(0, depth // strip)
        def _(at):
            here = pl.ds(pl.multiple_of(at * strip, strip), strip)
            turned = feat_rows[here].T
            token = lax.broadcasted_iota(jnp.int32, (rows, strip), 1) + at * strip
            owner = lax.div(lax.rem(token, live), live // batches)
            for batch in range(batches):
                feat_cols[batch, :, here] = jnp.where(owner == batch, turned, 0.0).astype(jnp.bfloat16)

    def hop(chunk, source, sem, way):
        return pltpu.make_async_remote_copy(
            src_ref=held.at[chunk, source],
            dst_ref=held.at[chunk, source],
            send_sem=sem.at[chunk, source],
            recv_sem=recv_sem.at[chunk, source],
            device_id=(dom, me + way * col_blocks),
            device_id_type=MESH,
        )

    def term_copy(chunk, peer_step, which):
        src, dst = ((numer, numer_in), (denom, denom_in))[which]
        peer = lax.rem(dom + peer_step, doms)
        return pltpu.make_async_remote_copy(
            src_ref=src.at[chunk, pl.ds(pl.multiple_of(peer * share, share), share)],
            dst_ref=dst.at[chunk, doms - 1 - peer_step],
            send_sem=term_send.at[chunk, peer_step - 1, which],
            recv_sem=term_recv.at[chunk, doms - 1 - peer_step, which],
            device_id=(peer, me),
            device_id_type=MESH,
        )

    def term_arrival(chunk, slot, which):
        dst = (numer_in, denom_in)[which]
        return pltpu.make_async_copy(dst.at[chunk, slot], dst.at[chunk, slot], term_recv.at[chunk, slot, which])

    def out_copy(chunk, peer_step):
        where = out.at[
            pl.ds(pl.multiple_of(dom * share, share), share), pl.ds(pl.multiple_of(chunk * width, width), width)
        ]
        return pltpu.make_async_remote_copy(
            src_ref=where,
            dst_ref=where,
            send_sem=out_send.at[chunk, peer_step - 1],
            recv_sem=out_recv.at[chunk, doms - 1 - peer_step],
            device_id=(lax.rem(dom + peer_step, doms), me),
            device_id_type=MESH,
        )

    def out_arrival(chunk, slot):
        peer = lax.rem(dom + slot + 1, doms)
        where = out.at[
            pl.ds(pl.multiple_of(peer * share, share), share), pl.ds(pl.multiple_of(chunk * width, width), width)
        ]
        return pltpu.make_async_copy(where, where, out_recv.at[chunk, slot])

    def compute(chunk):
        columns = pl.ds(pl.multiple_of(chunk * width, width), width)

        @pl.loop(0, rows // tile)
        def _(at):
            here = pl.ds(pl.multiple_of(at * tile, tile), tile)
            right = held[chunk].reshape(depth, width)
            total = None
            for batch in range(batches):
                grad = jnp.dot(feat_cols[batch, here], right, preferred_element_type=jnp.float32)
                total = grad * grad if total is None else total + grad * grad
            term = total / batches + damping
            denom[chunk, here] = term.astype(jnp.bfloat16)
            numer[chunk, here] = (term * weights[here, columns].astype(jnp.float32)).astype(jnp.bfloat16)

    def merge(chunk):
        columns = pl.ds(pl.multiple_of(chunk * width, width), width)

        @pl.loop(0, share // piece)
        def _(at):
            mine = pl.ds(pl.multiple_of(dom * share + at * piece, piece), piece)
            there = pl.ds(pl.multiple_of(at * piece, piece), piece)
            top = numer[chunk, mine].astype(jnp.float32)
            low = denom[chunk, mine].astype(jnp.float32)
            for slot in range(doms - 1):
                top = top + numer_in[chunk, slot, there].astype(jnp.float32)
                low = low + denom_in[chunk, slot, there].astype(jnp.float32)
            out[mine, columns] = (top / low).astype(jnp.bfloat16)

    def inside(chunk):
        return jnp.logical_and(chunk >= 0, chunk < chunks)

    ahead = min(2, chunks)
    for step in range(1, row_blocks):
        feat_along(step).start()
    for chunk in range(ahead):
        for step in range(1, col_blocks):
            piece_copy(chunk, step).start()
    feat_box[row] = feats[row]

    @pl.loop(0, chunks + row_blocks)
    def _(step):
        @pl.when(step + ahead < chunks)
        def _():
            for peer_step in range(1, col_blocks):
                piece_copy(step + ahead, peer_step).start()

        @pl.when(step < chunks)
        def _():
            for slot in range(col_blocks - 1):
                piece_arrival(step, slot).wait()
            assemble(step)

            @pl.when(row < last)
            def _():
                hop(step, row, up_sem, 1).start()

            @pl.when(row > 0)
            def _():
                hop(step, row, down_sem, -1).start()

        @pl.when(step == 0)
        def _():
            for slot in range(row_blocks - 1):
                feat_along_arrival(slot).wait()
            for peer_step in range(1, col_blocks):
                feat_across(peer_step).start()

        for far in range(1, row_blocks):
            chunk = step - far

            @pl.when(jnp.logical_and(inside(chunk), row - far >= 0))
            def _():
                hop(chunk, row - far, up_sem, 1).wait_recv()

                @pl.when(row < last)
                def _():
                    hop(chunk, row - far, up_sem, 1).start()

            @pl.when(jnp.logical_and(inside(chunk), row + far <= last))
            def _():
                hop(chunk, row + far, down_sem, -1).wait_recv()

                @pl.when(row > 0)
                def _():
                    hop(chunk, row + far, down_sem, -1).start()

        ready = step - last

        @pl.when(ready == 0)
        def _():
            for slot in range(col_blocks - 1):
                feat_across_arrival(slot).wait()
            turn_feats()

        @pl.when(inside(ready))
        def _():
            compute(ready)
            for peer_step in range(1, doms):
                for which in range(2):
                    term_copy(ready, peer_step, which).start()

        before = ready - 1

        @pl.when(inside(before))
        def _():
            for slot in range(doms - 1):
                for which in range(2):
                    term_arrival(before, slot, which).wait()
            merge(before)
            for peer_step in range(1, doms):
                out_copy(before, peer_step).start()

    for step in range(1, row_blocks):
        feat_along(step).wait_send()
    for step in range(1, col_blocks):
        feat_across(step).wait_send()

    @pl.loop(0, chunks)
    def _(chunk):
        for step in range(1, col_blocks):
            piece_copy(chunk, step).wait_send()
        for source in range(row_blocks):
            @pl.when(jnp.logical_and(row < last, source <= row))
            def _():
                hop(chunk, source, up_sem, 1).wait_send()

            @pl.when(jnp.logical_and(row > 0, source >= row))
            def _():
                hop(chunk, source, down_sem, -1).wait_send()

        for peer_step in range(1, doms):
            for which in range(2):
                term_copy(chunk, peer_step, which).wait_send()
            out_copy(chunk, peer_step).wait_send()
        for slot in range(doms - 1):
            out_arrival(chunk, slot).wait()


def chunk_width(cols):
    for width in (512, 384, 256, 128):
        if cols % width == 0:
            return width
    return cols


def body(weights, activations, cotangents, lengths):
    devices = lax.axis_size("fsdp")
    doms = lax.axis_size("dom")
    rows, cols = weights.shape[2:]
    batches, slots = activations.shape[1:3]
    row_blocks = activations.shape[3] // rows
    col_blocks = devices // row_blocks
    width = chunk_width(cols)
    chunks = cols // width
    tokens = col_blocks * batches * slots
    depth = row_blocks * tokens

    mask = (jnp.arange(slots)[None, :] < lengths[0, :, 0:1]).astype(jnp.bfloat16)
    feats = activations[0] * mask[:, :, None]
    live = batches * slots
    padded = -(-live // 16) * 16
    feats = feats.reshape(live, row_blocks, rows)
    feats = jnp.pad(feats, ((0, padded - live), (0, 0), (0, 0))).transpose(1, 0, 2)
    cots = cotangents[0].reshape(live, col_blocks, chunks, width)
    cots = jnp.pad(cots, ((0, padded - live), (0, 0), (0, 0), (0, 0))).transpose(1, 2, 0, 3)

    share = rows // doms
    vmem = pl.BlockSpec(memory_space=pltpu.VMEM)
    bf16 = jnp.bfloat16
    merged = pl.pallas_call(
        functools.partial(kernel, doms, row_blocks, col_blocks, live),
        out_shape=jax.ShapeDtypeStruct((rows, cols), bf16),
        in_specs=[vmem] * 3,
        out_specs=vmem,
        scratch_shapes=[
            pltpu.VMEM((row_blocks, padded, rows), bf16),
            pltpu.VMEM((col_blocks - 1, row_blocks, padded, rows), bf16),
            pltpu.VMEM((depth, rows), jnp.float32),
            pltpu.VMEM((batches, rows, depth), bf16),
            pltpu.VMEM((chunks, col_blocks - 1, padded, width), bf16),
            pltpu.VMEM((chunks, row_blocks, tokens, width), bf16),
            pltpu.VMEM((chunks, rows, width), bf16),
            pltpu.VMEM((chunks, rows, width), bf16),
            pltpu.VMEM((chunks, doms - 1, share, width), bf16),
            pltpu.VMEM((chunks, doms - 1, share, width), bf16),
            pltpu.SemaphoreType.DMA((row_blocks - 1,)),
            pltpu.SemaphoreType.DMA((row_blocks - 1,)),
            pltpu.SemaphoreType.DMA((col_blocks - 1,)),
            pltpu.SemaphoreType.DMA((col_blocks - 1,)),
            pltpu.SemaphoreType.DMA((chunks, col_blocks - 1)),
            pltpu.SemaphoreType.DMA((chunks, col_blocks - 1)),
            pltpu.SemaphoreType.DMA((chunks, row_blocks)),
            pltpu.SemaphoreType.DMA((chunks, row_blocks)),
            pltpu.SemaphoreType.DMA((chunks, row_blocks)),
            pltpu.SemaphoreType.DMA((chunks, doms - 1, 2)),
            pltpu.SemaphoreType.DMA((chunks, doms - 1, 2)),
            pltpu.SemaphoreType.DMA((chunks, doms - 1)),
            pltpu.SemaphoreType.DMA((chunks, doms - 1)),
        ],
        compiler_params=pltpu.CompilerParams(
            collective_id=0, has_side_effects=True, vmem_limit_bytes=56 << 20
        ),
    )(feats, cots, weights[0, 0])
    return merged[None]


def solution(mesh):
    return jax.shard_map(
        body,
        mesh=mesh,
        in_specs=(
            P("dom", "fsdp", None, None),
            P("dom", None, "fsdp", None),
            P("dom", None, "fsdp", None),
            P("dom", None, "fsdp"),
        ),
        out_specs=P("fsdp", None, None),
        check_vma=False,
    )
```

```python
import functools

import jax
import jax.numpy as jnp
from jax import lax
from jax.experimental import pallas as pl
from jax.experimental.pallas import tpu as pltpu
from jax.sharding import PartitionSpec as P

damping = 0.001
MESH = pl.DeviceIdType.MESH


def kernel(doms, row_blocks, col_blocks, live, feats, cots, weights_hbm, out, weights, feat_out, pieces, done,
           feat_box, feat_all, feat_rows, feat_cols, inbox, held, numer, denom, numer_in, denom_in,
           weight_sem, done_sem, along_send, along_recv, across_send, across_recv,
           piece_send, piece_recv, up_sem, down_sem, recv_sem, term_send, term_recv, out_send, out_recv):
    dom = lax.axis_index("dom")
    me = lax.axis_index("fsdp")
    row = lax.div(me, col_blocks)
    col = lax.rem(me, col_blocks)
    chunks, _, tokens, width = held.shape
    batches, rows, depth = feat_cols.shape
    share = rows // doms
    tile = 128 if rows % 128 == 0 else rows
    piece = 64 if share % 64 == 0 else share
    strip = 128 if depth % 128 == 0 else depth
    last = row_blocks - 1
    cols = chunks * width
    padded = pieces.shape[2]

    def fetch():
        return pltpu.make_async_copy(weights_hbm, weights, weight_sem)

    fetch().start()

    barrier = pltpu.get_barrier_semaphore()
    for step in range(1, row_blocks):
        other = lax.rem(me + step * col_blocks, row_blocks * col_blocks)
        pl.semaphore_signal(barrier, inc=1, device_id=(dom, other), device_id_type=MESH)
    for step in range(1, col_blocks):
        other = row * col_blocks + lax.rem(col + step, col_blocks)
        pl.semaphore_signal(barrier, inc=1, device_id=(dom, other), device_id_type=MESH)
    for step in range(1, doms):
        pl.semaphore_signal(barrier, inc=1, device_id=(lax.rem(dom + step, doms), me), device_id_type=MESH)
    pl.semaphore_wait(barrier, row_blocks - 1 + col_blocks - 1 + doms - 1)

    def feat_along(step):
        peer = lax.rem(row + step, row_blocks)
        return pltpu.make_async_remote_copy(
            src_ref=feat_out.at[peer],
            dst_ref=feat_box.at[row],
            send_sem=along_send.at[step - 1],
            recv_sem=along_recv.at[row_blocks - 1 - step],
            device_id=(dom, peer * col_blocks + col),
            device_id_type=MESH,
        )

    def feat_along_arrival(slot):
        dst = feat_box.at[lax.rem(row + slot + 1, row_blocks)]
        return pltpu.make_async_copy(dst, dst, along_recv.at[slot])

    def feat_across(step):
        return pltpu.make_async_remote_copy(
            src_ref=feat_box,
            dst_ref=feat_all.at[col_blocks - 1 - step],
            send_sem=across_send.at[step - 1],
            recv_sem=across_recv.at[col_blocks - 1 - step],
            device_id=(dom, row * col_blocks + lax.rem(col + step, col_blocks)),
            device_id_type=MESH,
        )

    def feat_across_arrival(slot):
        dst = feat_all.at[slot]
        return pltpu.make_async_copy(dst, dst, across_recv.at[slot])

    def piece_copy(chunk, step):
        peer = lax.rem(col + step, col_blocks)
        return pltpu.make_async_remote_copy(
            src_ref=pieces.at[chunk, step - 1],
            dst_ref=inbox.at[chunk, col_blocks - 1 - step],
            send_sem=piece_send.at[chunk, step - 1],
            recv_sem=piece_recv.at[chunk, col_blocks - 1 - step],
            device_id=(dom, row * col_blocks + peer),
            device_id_type=MESH,
        )

    def piece_arrival(chunk, slot):
        dst = inbox.at[chunk, slot]
        return pltpu.make_async_copy(dst, dst, piece_recv.at[chunk, slot])

    def join(parts):
        return jnp.concatenate([part.astype(jnp.float32)[:live] for part in parts], axis=0)

    def pad(part):
        if padded == live:
            return part
        blank = jnp.zeros((padded - live, part.shape[1]), jnp.float32)
        return jnp.concatenate([part.astype(jnp.float32), blank], axis=0).astype(jnp.bfloat16)

    def cot_part(chunk, block):
        return cots[:, pl.ds(pl.multiple_of(block * cols + chunk * width, width), width)]

    def feat_part(block):
        return pad(feats[:, pl.ds(pl.multiple_of(block * rows, rows), rows)])

    def send_pieces(chunk):
        for step in range(1, col_blocks):
            pieces[chunk, step - 1] = pad(cot_part(chunk, lax.rem(col + step, col_blocks)))
            piece_copy(chunk, step).start()

    def assemble(chunk):
        parts = [cot_part(chunk, col)] + [inbox[chunk, slot] for slot in range(col_blocks - 1)]
        held[chunk, row] = join(parts).astype(jnp.bfloat16)

    def turn_feats():
        @pl.loop(0, row_blocks)
        def _(at):
            parts = [feat_box[at]] + [feat_all[slot, at] for slot in range(col_blocks - 1)]
            feat_rows[pl.ds(pl.multiple_of(at * tokens, tokens), tokens)] = join(parts)

        @pl.loop(0, depth // strip)
        def _(at):
            here = pl.ds(pl.multiple_of(at * strip, strip), strip)
            turned = feat_rows[here].T
            token = lax.broadcasted_iota(jnp.int32, (rows, strip), 1) + at * strip
            owner = lax.rem(lax.rem(token, live), batches)
            for batch in range(batches):
                feat_cols[batch, :, here] = jnp.where(owner == batch, turned, 0.0).astype(jnp.bfloat16)

    def hop(chunk, source, sem, way):
        return pltpu.make_async_remote_copy(
            src_ref=held.at[chunk, source],
            dst_ref=held.at[chunk, source],
            send_sem=sem.at[chunk, source],
            recv_sem=recv_sem.at[chunk, source],
            device_id=(dom, me + way * col_blocks),
            device_id_type=MESH,
        )

    def term_copy(chunk, peer_step, which):
        src, dst = ((numer, numer_in), (denom, denom_in))[which]
        peer = lax.rem(dom + peer_step, doms)
        return pltpu.make_async_remote_copy(
            src_ref=src.at[chunk, pl.ds(pl.multiple_of(peer * share, share), share)],
            dst_ref=dst.at[chunk, doms - 1 - peer_step],
            send_sem=term_send.at[chunk, peer_step - 1, which],
            recv_sem=term_recv.at[chunk, doms - 1 - peer_step, which],
            device_id=(peer, me),
            device_id_type=MESH,
        )

    def term_arrival(chunk, slot, which):
        dst = (numer_in, denom_in)[which]
        return pltpu.make_async_copy(dst.at[chunk, slot], dst.at[chunk, slot], term_recv.at[chunk, slot, which])

    def place(owner, chunk):
        return out.at[
            pl.ds(pl.multiple_of(owner * share, share), share), pl.ds(pl.multiple_of(chunk * width, width), width)
        ]

    def keep(chunk):
        return pltpu.make_async_copy(done.at[chunk], place(dom, chunk), done_sem.at[chunk])

    def out_copy(chunk, peer_step):
        return pltpu.make_async_remote_copy(
            src_ref=done.at[chunk],
            dst_ref=place(dom, chunk),
            send_sem=out_send.at[chunk, peer_step - 1],
            recv_sem=out_recv.at[chunk, doms - 1 - peer_step],
            device_id=(lax.rem(dom + peer_step, doms), me),
            device_id_type=MESH,
        )

    def out_arrival(chunk, slot):
        where = place(lax.rem(dom + slot + 1, doms), chunk)
        return pltpu.make_async_copy(where, where, out_recv.at[chunk, slot])

    def compute(chunk):
        columns = pl.ds(pl.multiple_of(chunk * width, width), width)

        @pl.loop(0, rows // tile)
        def _(at):
            here = pl.ds(pl.multiple_of(at * tile, tile), tile)
            right = held[chunk].reshape(depth, width)
            total = None
            for batch in range(batches):
                grad = jnp.dot(feat_cols[batch, here], right, preferred_element_type=jnp.float32)
                total = grad * grad if total is None else total + grad * grad
            term = total / batches + damping
            denom[chunk, here] = term.astype(jnp.bfloat16)
            numer[chunk, here] = (term * weights[here, columns].astype(jnp.float32)).astype(jnp.bfloat16)

    def merge(chunk):
        @pl.loop(0, share // piece)
        def _(at):
            mine = pl.ds(pl.multiple_of(dom * share + at * piece, piece), piece)
            there = pl.ds(pl.multiple_of(at * piece, piece), piece)
            top = numer[chunk, mine].astype(jnp.float32)
            low = denom[chunk, mine].astype(jnp.float32)
            for slot in range(doms - 1):
                top = top + numer_in[chunk, slot, there].astype(jnp.float32)
                low = low + denom_in[chunk, slot, there].astype(jnp.float32)
            done[chunk, there] = (top / low).astype(jnp.bfloat16)

    def inside(chunk):
        return jnp.logical_and(chunk >= 0, chunk < chunks)

    ahead = min(2, chunks)
    for step in range(1, row_blocks):
        peer = lax.rem(row + step, row_blocks)
        feat_out[peer] = feat_part(peer)
        feat_along(step).start()
    for chunk in range(ahead):
        send_pieces(chunk)
    feat_box[row] = feat_part(row)

    @pl.loop(0, chunks + row_blocks)
    def _(step):
        @pl.when(step + ahead < chunks)
        def _():
            send_pieces(step + ahead)

        @pl.when(step < chunks)
        def _():
            for slot in range(col_blocks - 1):
                piece_arrival(step, slot).wait()
            assemble(step)

            @pl.when(row < last)
            def _():
                hop(step, row, up_sem, 1).start()

            @pl.when(row > 0)
            def _():
                hop(step, row, down_sem, -1).start()

        @pl.when(step == 0)
        def _():
            for slot in range(row_blocks - 1):
                feat_along_arrival(slot).wait()
            for peer_step in range(1, col_blocks):
                feat_across(peer_step).start()

        for far in range(1, row_blocks):
            chunk = step - far

            @pl.when(jnp.logical_and(inside(chunk), row - far >= 0))
            def _():
                hop(chunk, row - far, up_sem, 1).wait_recv()

                @pl.when(row < last)
                def _():
                    hop(chunk, row - far, up_sem, 1).start()

            @pl.when(jnp.logical_and(inside(chunk), row + far <= last))
            def _():
                hop(chunk, row + far, down_sem, -1).wait_recv()

                @pl.when(row > 0)
                def _():
                    hop(chunk, row + far, down_sem, -1).start()

        ready = step - last

        @pl.when(ready == 0)
        def _():
            for slot in range(col_blocks - 1):
                feat_across_arrival(slot).wait()
            turn_feats()
            fetch().wait()

        @pl.when(inside(ready))
        def _():
            compute(ready)
            for peer_step in range(1, doms):
                for which in range(2):
                    term_copy(ready, peer_step, which).start()

        before = ready - 1

        @pl.when(inside(before))
        def _():
            for slot in range(doms - 1):
                for which in range(2):
                    term_arrival(before, slot, which).wait()
            merge(before)
            keep(before).start()
            for peer_step in range(1, doms):
                out_copy(before, peer_step).start()

    for step in range(1, row_blocks):
        feat_along(step).wait_send()
    for step in range(1, col_blocks):
        feat_across(step).wait_send()

    @pl.loop(0, chunks)
    def _(chunk):
        for step in range(1, col_blocks):
            piece_copy(chunk, step).wait_send()
        for source in range(row_blocks):
            @pl.when(jnp.logical_and(row < last, source <= row))
            def _():
                hop(chunk, source, up_sem, 1).wait_send()

            @pl.when(jnp.logical_and(row > 0, source >= row))
            def _():
                hop(chunk, source, down_sem, -1).wait_send()

        for peer_step in range(1, doms):
            for which in range(2):
                term_copy(chunk, peer_step, which).wait_send()
            out_copy(chunk, peer_step).wait_send()
        keep(chunk).wait()
        for slot in range(doms - 1):
            out_arrival(chunk, slot).wait()


def chunk_width(cols):
    for width in (256, 128):
        if cols % width == 0:
            return width
    return cols


def body(weights, activations, cotangents, lengths):
    devices = lax.axis_size("fsdp")
    doms = lax.axis_size("dom")
    rows, cols = weights.shape[2:]
    batches, slots = activations.shape[1:3]
    row_blocks = activations.shape[3] // rows
    col_blocks = devices // row_blocks
    width = chunk_width(cols)
    chunks = cols // width
    tokens = col_blocks * batches * slots
    depth = row_blocks * tokens

    mask = (jnp.arange(slots)[:, None] < lengths[0, :, 0][None, :]).astype(jnp.bfloat16)
    live = batches * slots
    padded = -(-live // 16) * 16
    feats = (activations[0].transpose(1, 0, 2) * mask[:, :, None]).reshape(live, row_blocks * rows)
    cots = cotangents[0].transpose(1, 0, 2).reshape(live, col_blocks * cols)

    share = rows // doms
    vmem = pl.BlockSpec(memory_space=pltpu.VMEM)
    bf16 = jnp.bfloat16
    merged = pl.pallas_call(
        functools.partial(kernel, doms, row_blocks, col_blocks, live),
        out_shape=jax.ShapeDtypeStruct((rows, cols), bf16),
        in_specs=[vmem, vmem, pl.BlockSpec(memory_space=pl.ANY)],
        out_specs=pl.BlockSpec(memory_space=pl.ANY),
        scratch_shapes=[
            pltpu.VMEM((rows, cols), bf16),
            pltpu.VMEM((row_blocks, padded, rows), bf16),
            pltpu.VMEM((chunks, col_blocks - 1, padded, width), bf16),
            pltpu.VMEM((chunks, share, width), bf16),
            pltpu.VMEM((row_blocks, padded, rows), bf16),
            pltpu.VMEM((col_blocks - 1, row_blocks, padded, rows), bf16),
            pltpu.VMEM((depth, rows), jnp.float32),
            pltpu.VMEM((batches, rows, depth), bf16),
            pltpu.VMEM((chunks, col_blocks - 1, padded, width), bf16),
            pltpu.VMEM((chunks, row_blocks, tokens, width), bf16),
            pltpu.VMEM((chunks, rows, width), bf16),
            pltpu.VMEM((chunks, rows, width), bf16),
            pltpu.VMEM((chunks, doms - 1, share, width), bf16),
            pltpu.VMEM((chunks, doms - 1, share, width), bf16),
            pltpu.SemaphoreType.DMA,
            pltpu.SemaphoreType.DMA((chunks,)),
            pltpu.SemaphoreType.DMA((row_blocks - 1,)),
            pltpu.SemaphoreType.DMA((row_blocks - 1,)),
            pltpu.SemaphoreType.DMA((col_blocks - 1,)),
            pltpu.SemaphoreType.DMA((col_blocks - 1,)),
            pltpu.SemaphoreType.DMA((chunks, col_blocks - 1)),
            pltpu.SemaphoreType.DMA((chunks, col_blocks - 1)),
            pltpu.SemaphoreType.DMA((chunks, row_blocks)),
            pltpu.SemaphoreType.DMA((chunks, row_blocks)),
            pltpu.SemaphoreType.DMA((chunks, row_blocks)),
            pltpu.SemaphoreType.DMA((chunks, doms - 1, 2)),
            pltpu.SemaphoreType.DMA((chunks, doms - 1, 2)),
            pltpu.SemaphoreType.DMA((chunks, doms - 1)),
            pltpu.SemaphoreType.DMA((chunks, doms - 1)),
        ],
        compiler_params=pltpu.CompilerParams(
            collective_id=0, has_side_effects=True, vmem_limit_bytes=44 << 20
        ),
    )(feats, cots, weights[0, 0])
    return merged[None]


def solution(mesh):
    return jax.shard_map(
        body,
        mesh=mesh,
        in_specs=(
            P("dom", "fsdp", None, None),
            P("dom", None, "fsdp", None),
            P("dom", None, "fsdp", None),
            P("dom", None, "fsdp"),
        ),
        out_specs=P("fsdp", None, None),
        check_vma=False,
    )
```

```python
import functools

import jax
import jax.numpy as jnp
from jax import lax
from jax.experimental import pallas as pl
from jax.experimental.pallas import tpu as pltpu
from jax.sharding import PartitionSpec as P

damping = 0.001
MESH = pl.DeviceIdType.MESH


def kernel(doms, row_blocks, col_blocks, live, feats, cots, weights_hbm, out, weights, feat_out, pieces, done,
           feat_box, feat_all, feat_rows, feat_cols, inbox, held, numer, denom, numer_in, denom_in,
           weight_sem, done_sem, along_send, along_recv, across_send, across_recv,
           piece_send, piece_recv, up_sem, down_sem, recv_sem, term_send, term_recv, out_send, out_recv):
    dom = lax.axis_index("dom")
    me = lax.axis_index("fsdp")
    row = lax.div(me, col_blocks)
    col = lax.rem(me, col_blocks)
    chunks, _, tokens, width = held.shape
    batches, rows, depth = feat_cols.shape
    share = rows // doms
    tile = 320 if share % 320 == 0 else share
    piece = 64 if share % 64 == 0 else share
    strip = 128 if depth % 128 == 0 else depth
    last = row_blocks - 1
    cols = chunks * width
    parts, _, thin = numer.shape
    halves = parts // chunks
    padded = pieces.shape[2]

    def fetch():
        return pltpu.make_async_copy(weights_hbm, weights, weight_sem)

    fetch().start()

    barrier = pltpu.get_barrier_semaphore()
    for step in range(1, row_blocks):
        other = lax.rem(me + step * col_blocks, row_blocks * col_blocks)
        pl.semaphore_signal(barrier, inc=1, device_id=(dom, other), device_id_type=MESH)
    for step in range(1, col_blocks):
        other = row * col_blocks + lax.rem(col + step, col_blocks)
        pl.semaphore_signal(barrier, inc=1, device_id=(dom, other), device_id_type=MESH)
    for step in range(1, doms):
        pl.semaphore_signal(barrier, inc=1, device_id=(lax.rem(dom + step, doms), me), device_id_type=MESH)
    pl.semaphore_wait(barrier, row_blocks - 1 + col_blocks - 1 + doms - 1)

    def feat_along(step):
        peer = lax.rem(row + step, row_blocks)
        return pltpu.make_async_remote_copy(
            src_ref=feat_out.at[peer],
            dst_ref=feat_box.at[row],
            send_sem=along_send.at[step - 1],
            recv_sem=along_recv.at[row_blocks - 1 - step],
            device_id=(dom, peer * col_blocks + col),
            device_id_type=MESH,
        )

    def feat_along_arrival(slot):
        dst = feat_box.at[lax.rem(row + slot + 1, row_blocks)]
        return pltpu.make_async_copy(dst, dst, along_recv.at[slot])

    def feat_across(step):
        return pltpu.make_async_remote_copy(
            src_ref=feat_box,
            dst_ref=feat_all.at[col_blocks - 1 - step],
            send_sem=across_send.at[step - 1],
            recv_sem=across_recv.at[col_blocks - 1 - step],
            device_id=(dom, row * col_blocks + lax.rem(col + step, col_blocks)),
            device_id_type=MESH,
        )

    def feat_across_arrival(slot):
        dst = feat_all.at[slot]
        return pltpu.make_async_copy(dst, dst, across_recv.at[slot])

    def piece_copy(chunk, step):
        peer = lax.rem(col + step, col_blocks)
        return pltpu.make_async_remote_copy(
            src_ref=pieces.at[chunk, step - 1],
            dst_ref=inbox.at[chunk, col_blocks - 1 - step],
            send_sem=piece_send.at[chunk, step - 1],
            recv_sem=piece_recv.at[chunk, col_blocks - 1 - step],
            device_id=(dom, row * col_blocks + peer),
            device_id_type=MESH,
        )

    def piece_arrival(chunk, slot):
        dst = inbox.at[chunk, slot]
        return pltpu.make_async_copy(dst, dst, piece_recv.at[chunk, slot])

    def join(parts):
        return jnp.concatenate([part.astype(jnp.float32)[:live] for part in parts], axis=0)

    def pad(part):
        if padded == live:
            return part.astype(jnp.bfloat16)
        blank = jnp.zeros((padded - live, part.shape[1]), jnp.float32)
        return jnp.concatenate([part.astype(jnp.float32), blank], axis=0).astype(jnp.bfloat16)

    def cot_part(chunk, block):
        where = pl.ds(pl.multiple_of(block * cols + chunk * width, width), width)
        return jnp.concatenate([cots[batch, :, where].astype(jnp.float32) for batch in range(batches)], axis=0)

    def feat_part(block):
        return pad(feats[:, pl.ds(pl.multiple_of(block * rows, rows), rows)])

    def send_pieces(chunk):
        for step in range(1, col_blocks):
            pieces[chunk, step - 1] = pad(cot_part(chunk, lax.rem(col + step, col_blocks)))
            piece_copy(chunk, step).start()

    def assemble(chunk):
        parts = [cot_part(chunk, col)] + [inbox[chunk, slot] for slot in range(col_blocks - 1)]
        held[chunk, row] = join(parts).astype(jnp.bfloat16)

    def turn_feats():
        @pl.loop(0, row_blocks)
        def _(at):
            parts = [feat_box[at]] + [feat_all[slot, at] for slot in range(col_blocks - 1)]
            feat_rows[pl.ds(pl.multiple_of(at * tokens, tokens), tokens)] = join(parts)

        @pl.loop(0, depth // strip)
        def _(at):
            here = pl.ds(pl.multiple_of(at * strip, strip), strip)
            turned = feat_rows[here].T
            token = lax.broadcasted_iota(jnp.int32, (rows, strip), 1) + at * strip
            owner = lax.div(lax.rem(token, live), live // batches)
            for batch in range(batches):
                feat_cols[batch, :, here] = jnp.where(owner == batch, turned, 0.0).astype(jnp.bfloat16)

    def hop(chunk, source, sem, way):
        return pltpu.make_async_remote_copy(
            src_ref=held.at[chunk, source],
            dst_ref=held.at[chunk, source],
            send_sem=sem.at[chunk, source],
            recv_sem=recv_sem.at[chunk, source],
            device_id=(dom, me + way * col_blocks),
            device_id_type=MESH,
        )

    def term_copy(chunk, peer_step, which):
        src, dst = ((numer, numer_in), (denom, denom_in))[which]
        peer = lax.rem(dom + peer_step, doms)
        return pltpu.make_async_remote_copy(
            src_ref=src.at[chunk, pl.ds(pl.multiple_of(peer * share, share), share)],
            dst_ref=dst.at[chunk, doms - 1 - peer_step],
            send_sem=term_send.at[chunk, peer_step - 1, which],
            recv_sem=term_recv.at[chunk, doms - 1 - peer_step, which],
            device_id=(peer, me),
            device_id_type=MESH,
        )

    def term_arrival(chunk, slot, which):
        dst = (numer_in, denom_in)[which]
        return pltpu.make_async_copy(dst.at[chunk, slot], dst.at[chunk, slot], term_recv.at[chunk, slot, which])

    def place(owner, chunk):
        return out.at[
            pl.ds(pl.multiple_of(owner * share, share), share), pl.ds(pl.multiple_of(chunk * thin, thin), thin)
        ]

    def keep(chunk):
        return pltpu.make_async_copy(done.at[chunk], place(dom, chunk), done_sem.at[chunk])

    def out_copy(chunk, peer_step):
        return pltpu.make_async_remote_copy(
            src_ref=done.at[chunk],
            dst_ref=place(dom, chunk),
            send_sem=out_send.at[chunk, peer_step - 1],
            recv_sem=out_recv.at[chunk, doms - 1 - peer_step],
            device_id=(lax.rem(dom + peer_step, doms), me),
            device_id_type=MESH,
        )

    def out_arrival(chunk, slot):
        where = place(lax.rem(dom + slot + 1, doms), chunk)
        return pltpu.make_async_copy(where, where, out_recv.at[chunk, slot])

    def compute(whole, half, owner):
        chunk = whole * halves + half
        columns = pl.ds(pl.multiple_of(chunk * thin, thin), thin)

        @pl.loop(0, share // tile)
        def _(at):
            here = pl.ds(pl.multiple_of(owner * share + at * tile, tile), tile)
            right = held[whole, :, :, half * thin : (half + 1) * thin].reshape(depth, thin)
            total = None
            for batch in range(batches):
                grad = jnp.dot(feat_cols[batch, here], right, preferred_element_type=jnp.float32)
                total = grad * grad if total is None else total + grad * grad
            term = total / batches + damping
            denom[chunk, here] = term.astype(jnp.bfloat16)
            numer[chunk, here] = (term * weights[here, columns].astype(jnp.float32)).astype(jnp.bfloat16)

    def merge(chunk):
        @pl.loop(0, share // piece)
        def _(at):
            mine = pl.ds(pl.multiple_of(dom * share + at * piece, piece), piece)
            there = pl.ds(pl.multiple_of(at * piece, piece), piece)
            top = numer[chunk, mine].astype(jnp.float32)
            low = denom[chunk, mine].astype(jnp.float32)
            for slot in range(doms - 1):
                top = top + numer_in[chunk, slot, there].astype(jnp.float32)
                low = low + denom_in[chunk, slot, there].astype(jnp.float32)
            done[chunk, there] = (top / low).astype(jnp.bfloat16)

    def inside(chunk):
        return jnp.logical_and(chunk >= 0, chunk < chunks)

    ahead = min(2, chunks)
    for step in range(1, row_blocks):
        peer = lax.rem(row + step, row_blocks)
        feat_out[peer] = feat_part(peer)
        feat_along(step).start()
    for chunk in range(ahead):
        send_pieces(chunk)
    feat_box[row] = feat_part(row)

    @pl.loop(0, chunks + row_blocks)
    def _(step):
        @pl.when(step + ahead < chunks)
        def _():
            send_pieces(step + ahead)

        @pl.when(step < chunks)
        def _():
            for slot in range(col_blocks - 1):
                piece_arrival(step, slot).wait()
            assemble(step)

            @pl.when(row < last)
            def _():
                hop(step, row, up_sem, 1).start()

            @pl.when(row > 0)
            def _():
                hop(step, row, down_sem, -1).start()

        @pl.when(step == 0)
        def _():
            for slot in range(row_blocks - 1):
                feat_along_arrival(slot).wait()
            for peer_step in range(1, col_blocks):
                feat_across(peer_step).start()

        for half in range(halves):
            before = (step - row_blocks) * halves + half

            @pl.when(jnp.logical_and(before >= 0, before < parts))
            def _():
                for slot in range(doms - 1):
                    for which in range(2):
                        term_arrival(before, slot, which).wait()
                merge(before)
                keep(before).start()
                for peer_step in range(1, doms):
                    out_copy(before, peer_step).start()

        for far in range(1, row_blocks):
            chunk = step - far

            @pl.when(jnp.logical_and(inside(chunk), row - far >= 0))
            def _():
                hop(chunk, row - far, up_sem, 1).wait_recv()

                @pl.when(row < last)
                def _():
                    hop(chunk, row - far, up_sem, 1).start()

            @pl.when(jnp.logical_and(inside(chunk), row + far <= last))
            def _():
                hop(chunk, row + far, down_sem, -1).wait_recv()

                @pl.when(row > 0)
                def _():
                    hop(chunk, row + far, down_sem, -1).start()

        ready = step - last

        @pl.when(ready == 0)
        def _():
            for slot in range(col_blocks - 1):
                feat_across_arrival(slot).wait()
            turn_feats()
            fetch().wait()

        for half in range(halves):
            part = ready * halves + half

            @pl.when(inside(ready))
            def _():
                for peer_step in range(1, doms):
                    compute(ready, half, lax.rem(dom + peer_step, doms))
                    for which in range(2):
                        term_copy(part, peer_step, which).start()
                compute(ready, half, dom)

    for step in range(1, row_blocks):
        feat_along(step).wait_send()
    for step in range(1, col_blocks):
        feat_across(step).wait_send()

    @pl.loop(0, chunks)
    def _(chunk):
        for step in range(1, col_blocks):
            piece_copy(chunk, step).wait_send()
        for source in range(row_blocks):
            @pl.when(jnp.logical_and(row < last, source <= row))
            def _():
                hop(chunk, source, up_sem, 1).wait_send()

            @pl.when(jnp.logical_and(row > 0, source >= row))
            def _():
                hop(chunk, source, down_sem, -1).wait_send()

    @pl.loop(0, parts)
    def _(chunk):
        for peer_step in range(1, doms):
            for which in range(2):
                term_copy(chunk, peer_step, which).wait_send()
            out_copy(chunk, peer_step).wait_send()
        keep(chunk).wait()
        for slot in range(doms - 1):
            out_arrival(chunk, slot).wait()


def chunk_width(cols):
    for width in (512, 256, 128):
        if cols % width == 0:
            return width
    return cols


def body(weights, activations, cotangents, lengths):
    devices = lax.axis_size("fsdp")
    doms = lax.axis_size("dom")
    rows, cols = weights.shape[2:]
    batches, slots = activations.shape[1:3]
    row_blocks = activations.shape[3] // rows
    col_blocks = devices // row_blocks
    width = chunk_width(cols)
    chunks = cols // width
    halves = 2 if width % 256 == 0 else 1
    parts, thin = chunks * halves, width // halves
    tokens = col_blocks * batches * slots
    depth = row_blocks * tokens

    mask = (jnp.arange(slots)[None, :] < lengths[0, :, 0:1]).astype(jnp.bfloat16)
    live = batches * slots
    padded = -(-live // 16) * 16
    feats = (activations[0] * mask[:, :, None]).reshape(live, row_blocks * rows)
    cots = cotangents[0]

    share = rows // doms
    vmem = pl.BlockSpec(memory_space=pltpu.VMEM)
    bf16 = jnp.bfloat16
    merged = pl.pallas_call(
        functools.partial(kernel, doms, row_blocks, col_blocks, live),
        out_shape=jax.ShapeDtypeStruct((rows, cols), bf16),
        in_specs=[vmem, vmem, pl.BlockSpec(memory_space=pl.ANY)],
        out_specs=pl.BlockSpec(memory_space=pl.ANY),
        scratch_shapes=[
            pltpu.VMEM((rows, cols), bf16),
            pltpu.VMEM((row_blocks, padded, rows), bf16),
            pltpu.VMEM((chunks, col_blocks - 1, padded, width), bf16),
            pltpu.VMEM((parts, share, thin), bf16),
            pltpu.VMEM((row_blocks, padded, rows), bf16),
            pltpu.VMEM((col_blocks - 1, row_blocks, padded, rows), bf16),
            pltpu.VMEM((depth, rows), jnp.float32),
            pltpu.VMEM((batches, rows, depth), bf16),
            pltpu.VMEM((chunks, col_blocks - 1, padded, width), bf16),
            pltpu.VMEM((chunks, row_blocks, tokens, width), bf16),
            pltpu.VMEM((parts, rows, thin), bf16),
            pltpu.VMEM((parts, rows, thin), bf16),
            pltpu.VMEM((parts, doms - 1, share, thin), bf16),
            pltpu.VMEM((parts, doms - 1, share, thin), bf16),
            pltpu.SemaphoreType.DMA,
            pltpu.SemaphoreType.DMA((parts,)),
            pltpu.SemaphoreType.DMA((row_blocks - 1,)),
            pltpu.SemaphoreType.DMA((row_blocks - 1,)),
            pltpu.SemaphoreType.DMA((col_blocks - 1,)),
            pltpu.SemaphoreType.DMA((col_blocks - 1,)),
            pltpu.SemaphoreType.DMA((chunks, col_blocks - 1)),
            pltpu.SemaphoreType.DMA((chunks, col_blocks - 1)),
            pltpu.SemaphoreType.DMA((chunks, row_blocks)),
            pltpu.SemaphoreType.DMA((chunks, row_blocks)),
            pltpu.SemaphoreType.DMA((chunks, row_blocks)),
            pltpu.SemaphoreType.DMA((parts, doms - 1, 2)),
            pltpu.SemaphoreType.DMA((parts, doms - 1, 2)),
            pltpu.SemaphoreType.DMA((parts, doms - 1)),
            pltpu.SemaphoreType.DMA((parts, doms - 1)),
        ],
        compiler_params=pltpu.CompilerParams(
            collective_id=0, has_side_effects=True, vmem_limit_bytes=44 << 20
        ),
    )(feats, cots, weights[0, 0])
    return merged[None]


def solution(mesh):
    return jax.shard_map(
        body,
        mesh=mesh,
        in_specs=(
            P("dom", "fsdp", None, None),
            P("dom", None, "fsdp", None),
            P("dom", None, "fsdp", None),
            P("dom", None, "fsdp"),
        ),
        out_specs=P("fsdp", None, None),
        check_vma=False,
    )
```

```python
import functools

import jax
import jax.numpy as jnp
from jax import lax
from jax.experimental import pallas as pl
from jax.experimental.pallas import tpu as pltpu
from jax.sharding import PartitionSpec as P

damping = 0.001
MESH = pl.DeviceIdType.MESH


def kernel(doms, row_blocks, col_blocks, live, feats, cots, weights_hbm, out, weights, feat_out, pieces, done,
           feat_box, feat_all, feat_rows, feat_cols, inbox, held, numer, denom, numer_in, denom_in,
           weight_sem, done_sem, along_send, along_recv, across_send, across_recv,
           piece_send, piece_recv, up_sem, down_sem, recv_sem, term_send, term_recv, out_send, out_recv):
    dom = lax.axis_index("dom")
    me = lax.axis_index("fsdp")
    row = lax.div(me, col_blocks)
    col = lax.rem(me, col_blocks)
    chunks, _, tokens, width = held.shape
    batches, rows, depth = feat_cols.shape
    share = rows // doms
    tile = 320 if share % 320 == 0 else share
    piece = 64 if share % 64 == 0 else share
    strip = 128 if depth % 128 == 0 else depth
    last = row_blocks - 1
    cols = chunks * width
    parts, _, thin = numer.shape
    halves = parts // chunks
    padded = pieces.shape[2]

    def fetch():
        return pltpu.make_async_copy(weights_hbm, weights, weight_sem)

    fetch().start()

    barrier = pltpu.get_barrier_semaphore()
    for step in range(1, row_blocks):
        other = lax.rem(me + step * col_blocks, row_blocks * col_blocks)
        pl.semaphore_signal(barrier, inc=1, device_id=(dom, other), device_id_type=MESH)
    for step in range(1, col_blocks):
        other = row * col_blocks + lax.rem(col + step, col_blocks)
        pl.semaphore_signal(barrier, inc=1, device_id=(dom, other), device_id_type=MESH)
    for step in range(1, doms):
        pl.semaphore_signal(barrier, inc=1, device_id=(lax.rem(dom + step, doms), me), device_id_type=MESH)
    pl.semaphore_wait(barrier, row_blocks - 1 + col_blocks - 1 + doms - 1)

    def feat_along(step):
        peer = lax.rem(row + step, row_blocks)
        return pltpu.make_async_remote_copy(
            src_ref=feat_out.at[peer],
            dst_ref=feat_box.at[row],
            send_sem=along_send.at[step - 1],
            recv_sem=along_recv.at[row_blocks - 1 - step],
            device_id=(dom, peer * col_blocks + col),
            device_id_type=MESH,
        )

    def feat_along_arrival(slot):
        dst = feat_box.at[lax.rem(row + slot + 1, row_blocks)]
        return pltpu.make_async_copy(dst, dst, along_recv.at[slot])

    def feat_across(step):
        return pltpu.make_async_remote_copy(
            src_ref=feat_box,
            dst_ref=feat_all.at[col_blocks - 1 - step],
            send_sem=across_send.at[step - 1],
            recv_sem=across_recv.at[col_blocks - 1 - step],
            device_id=(dom, row * col_blocks + lax.rem(col + step, col_blocks)),
            device_id_type=MESH,
        )

    def feat_across_arrival(slot):
        dst = feat_all.at[slot]
        return pltpu.make_async_copy(dst, dst, across_recv.at[slot])

    def piece_copy(chunk, step):
        peer = lax.rem(col + step, col_blocks)
        return pltpu.make_async_remote_copy(
            src_ref=pieces.at[chunk, step - 1],
            dst_ref=inbox.at[chunk, col_blocks - 1 - step],
            send_sem=piece_send.at[chunk, step - 1],
            recv_sem=piece_recv.at[chunk, col_blocks - 1 - step],
            device_id=(dom, row * col_blocks + peer),
            device_id_type=MESH,
        )

    def piece_arrival(chunk, slot):
        dst = inbox.at[chunk, slot]
        return pltpu.make_async_copy(dst, dst, piece_recv.at[chunk, slot])

    def join(parts):
        return jnp.concatenate([part.astype(jnp.float32)[:live] for part in parts], axis=0)

    def pad(part):
        if padded == live:
            return part.astype(jnp.bfloat16)
        blank = jnp.zeros((padded - live, part.shape[1]), jnp.float32)
        return jnp.concatenate([part.astype(jnp.float32), blank], axis=0).astype(jnp.bfloat16)

    def cot_part(chunk, block):
        where = pl.ds(pl.multiple_of(block * cols + chunk * width, width), width)
        return jnp.concatenate([cots[batch, :, where].astype(jnp.float32) for batch in range(batches)], axis=0)

    def feat_part(block):
        return pad(feats[:, pl.ds(pl.multiple_of(block * rows, rows), rows)])

    def send_pieces(chunk):
        for step in range(1, col_blocks):
            pieces[chunk, step - 1] = pad(cot_part(chunk, lax.rem(col + step, col_blocks)))
            piece_copy(chunk, step).start()

    def assemble(chunk):
        parts = [cot_part(chunk, col)] + [inbox[chunk, slot] for slot in range(col_blocks - 1)]
        held[chunk, row] = join(parts).astype(jnp.bfloat16)

    def turn_feats():
        @pl.loop(0, row_blocks)
        def _(at):
            parts = [feat_box[at]] + [feat_all[slot, at] for slot in range(col_blocks - 1)]
            feat_rows[pl.ds(pl.multiple_of(at * tokens, tokens), tokens)] = join(parts)

        @pl.loop(0, depth // strip)
        def _(at):
            here = pl.ds(pl.multiple_of(at * strip, strip), strip)
            turned = feat_rows[here].T
            token = lax.broadcasted_iota(jnp.int32, (rows, strip), 1) + at * strip
            owner = lax.div(lax.rem(token, live), live // batches)
            for batch in range(batches):
                feat_cols[batch, :, here] = jnp.where(owner == batch, turned, 0.0).astype(jnp.bfloat16)

    def hop(chunk, source, sem, way):
        return pltpu.make_async_remote_copy(
            src_ref=held.at[chunk, source],
            dst_ref=held.at[chunk, source],
            send_sem=sem.at[chunk, source],
            recv_sem=recv_sem.at[chunk, source],
            device_id=(dom, me + way * col_blocks),
            device_id_type=MESH,
        )

    def term_copy(chunk, peer_step, which):
        src, dst = ((numer, numer_in), (denom, denom_in))[which]
        peer = lax.rem(dom + peer_step, doms)
        return pltpu.make_async_remote_copy(
            src_ref=src.at[chunk, pl.ds(pl.multiple_of(peer * share, share), share)],
            dst_ref=dst.at[chunk, doms - 1 - peer_step],
            send_sem=term_send.at[chunk, peer_step - 1, which],
            recv_sem=term_recv.at[chunk, doms - 1 - peer_step, which],
            device_id=(peer, me),
            device_id_type=MESH,
        )

    def term_arrival(chunk, slot, which):
        dst = (numer_in, denom_in)[which]
        return pltpu.make_async_copy(dst.at[chunk, slot], dst.at[chunk, slot], term_recv.at[chunk, slot, which])

    def place(owner, chunk):
        return out.at[
            pl.ds(pl.multiple_of(owner * share, share), share), pl.ds(pl.multiple_of(chunk * thin, thin), thin)
        ]

    def keep(chunk):
        return pltpu.make_async_copy(done.at[chunk], place(dom, chunk), done_sem.at[chunk])

    def out_copy(chunk, peer_step):
        return pltpu.make_async_remote_copy(
            src_ref=done.at[chunk],
            dst_ref=place(dom, chunk),
            send_sem=out_send.at[chunk, peer_step - 1],
            recv_sem=out_recv.at[chunk, doms - 1 - peer_step],
            device_id=(lax.rem(dom + peer_step, doms), me),
            device_id_type=MESH,
        )

    def out_arrival(chunk, slot):
        where = place(lax.rem(dom + slot + 1, doms), chunk)
        return pltpu.make_async_copy(where, where, out_recv.at[chunk, slot])

    def compute(whole, half, owner):
        chunk = whole * halves + half
        columns = pl.ds(pl.multiple_of(chunk * thin, thin), thin)

        @pl.loop(0, share // tile)
        def _(at):
            here = pl.ds(pl.multiple_of(owner * share + at * tile, tile), tile)
            right = held[whole, :, :, half * thin : (half + 1) * thin].reshape(depth, thin)
            total = None
            for batch in range(batches):
                grad = jnp.dot(feat_cols[batch, here], right, preferred_element_type=jnp.float32)
                total = grad * grad if total is None else total + grad * grad
            term = total / batches + damping
            denom[chunk, here] = term.astype(jnp.bfloat16)
            numer[chunk, here] = (term * weights[here, columns].astype(jnp.float32)).astype(jnp.bfloat16)

    def merge(chunk):
        @pl.loop(0, share // piece)
        def _(at):
            mine = pl.ds(pl.multiple_of(dom * share + at * piece, piece), piece)
            there = pl.ds(pl.multiple_of(at * piece, piece), piece)
            top = numer[chunk, mine].astype(jnp.float32)
            low = denom[chunk, mine].astype(jnp.float32)
            for slot in range(doms - 1):
                top = top + numer_in[chunk, slot, there].astype(jnp.float32)
                low = low + denom_in[chunk, slot, there].astype(jnp.float32)
            done[chunk, there] = (top / low).astype(jnp.bfloat16)

    def inside(chunk):
        return jnp.logical_and(chunk >= 0, chunk < chunks)

    ahead = min(2, chunks)
    send_pieces(0)
    for step in range(1, row_blocks):
        peer = lax.rem(row + step, row_blocks)
        feat_out[peer] = feat_part(peer)
        feat_along(step).start()
    for chunk in range(1, ahead):
        send_pieces(chunk)
    feat_box[row] = feat_part(row)

    @pl.loop(0, chunks + row_blocks)
    def _(step):
        @pl.when(step + ahead < chunks)
        def _():
            send_pieces(step + ahead)

        @pl.when(step < chunks)
        def _():
            for slot in range(col_blocks - 1):
                piece_arrival(step, slot).wait()
            assemble(step)

            @pl.when(row < last)
            def _():
                hop(step, row, up_sem, 1).start()

            @pl.when(row > 0)
            def _():
                hop(step, row, down_sem, -1).start()

        @pl.when(step == 1)
        def _():
            for slot in range(row_blocks - 1):
                feat_along_arrival(slot).wait()
            for peer_step in range(1, col_blocks):
                feat_across(peer_step).start()

        for half in range(halves):
            before = (step - row_blocks) * halves + half

            @pl.when(jnp.logical_and(before >= 0, before < parts))
            def _():
                for slot in range(doms - 1):
                    for which in range(2):
                        term_arrival(before, slot, which).wait()
                merge(before)
                keep(before).start()
                for peer_step in range(1, doms):
                    out_copy(before, peer_step).start()

        for far in range(1, row_blocks):
            chunk = step - far

            @pl.when(jnp.logical_and(inside(chunk), row - far >= 0))
            def _():
                hop(chunk, row - far, up_sem, 1).wait_recv()

                @pl.when(row < last)
                def _():
                    hop(chunk, row - far, up_sem, 1).start()

            @pl.when(jnp.logical_and(inside(chunk), row + far <= last))
            def _():
                hop(chunk, row + far, down_sem, -1).wait_recv()

                @pl.when(row > 0)
                def _():
                    hop(chunk, row + far, down_sem, -1).start()

        ready = step - last

        @pl.when(ready == 0)
        def _():
            for slot in range(col_blocks - 1):
                feat_across_arrival(slot).wait()
            turn_feats()
            fetch().wait()

        for half in range(halves):
            part = ready * halves + half

            @pl.when(inside(ready))
            def _():
                for peer_step in range(1, doms):
                    compute(ready, half, lax.rem(dom + peer_step, doms))
                    for which in range(2):
                        term_copy(part, peer_step, which).start()
                compute(ready, half, dom)

    for step in range(1, row_blocks):
        feat_along(step).wait_send()
    for step in range(1, col_blocks):
        feat_across(step).wait_send()

    @pl.loop(0, chunks)
    def _(chunk):
        for step in range(1, col_blocks):
            piece_copy(chunk, step).wait_send()
        for source in range(row_blocks):
            @pl.when(jnp.logical_and(row < last, source <= row))
            def _():
                hop(chunk, source, up_sem, 1).wait_send()

            @pl.when(jnp.logical_and(row > 0, source >= row))
            def _():
                hop(chunk, source, down_sem, -1).wait_send()

    @pl.loop(0, parts)
    def _(chunk):
        for peer_step in range(1, doms):
            for which in range(2):
                term_copy(chunk, peer_step, which).wait_send()
            out_copy(chunk, peer_step).wait_send()
        keep(chunk).wait()
        for slot in range(doms - 1):
            out_arrival(chunk, slot).wait()


def chunk_width(cols):
    for width in (512, 256, 128):
        if cols % width == 0:
            return width
    return cols


def body(weights, activations, cotangents, lengths):
    devices = lax.axis_size("fsdp")
    doms = lax.axis_size("dom")
    rows, cols = weights.shape[2:]
    batches, slots = activations.shape[1:3]
    row_blocks = activations.shape[3] // rows
    col_blocks = devices // row_blocks
    width = chunk_width(cols)
    chunks = cols // width
    halves = 2 if width % 256 == 0 else 1
    parts, thin = chunks * halves, width // halves
    tokens = col_blocks * batches * slots
    depth = row_blocks * tokens

    mask = (jnp.arange(slots)[None, :] < lengths[0, :, 0:1]).astype(jnp.bfloat16)
    live = batches * slots
    padded = -(-live // 16) * 16
    feats = (activations[0] * mask[:, :, None]).reshape(live, row_blocks * rows)
    cots = cotangents[0]

    share = rows // doms
    vmem = pl.BlockSpec(memory_space=pltpu.VMEM)
    bf16 = jnp.bfloat16
    merged = pl.pallas_call(
        functools.partial(kernel, doms, row_blocks, col_blocks, live),
        out_shape=jax.ShapeDtypeStruct((rows, cols), bf16),
        in_specs=[vmem, vmem, pl.BlockSpec(memory_space=pl.ANY)],
        out_specs=pl.BlockSpec(memory_space=pl.ANY),
        scratch_shapes=[
            pltpu.VMEM((rows, cols), bf16),
            pltpu.VMEM((row_blocks, padded, rows), bf16),
            pltpu.VMEM((chunks, col_blocks - 1, padded, width), bf16),
            pltpu.VMEM((parts, share, thin), bf16),
            pltpu.VMEM((row_blocks, padded, rows), bf16),
            pltpu.VMEM((col_blocks - 1, row_blocks, padded, rows), bf16),
            pltpu.VMEM((depth, rows), jnp.float32),
            pltpu.VMEM((batches, rows, depth), bf16),
            pltpu.VMEM((chunks, col_blocks - 1, padded, width), bf16),
            pltpu.VMEM((chunks, row_blocks, tokens, width), bf16),
            pltpu.VMEM((parts, rows, thin), bf16),
            pltpu.VMEM((parts, rows, thin), bf16),
            pltpu.VMEM((parts, doms - 1, share, thin), bf16),
            pltpu.VMEM((parts, doms - 1, share, thin), bf16),
            pltpu.SemaphoreType.DMA,
            pltpu.SemaphoreType.DMA((parts,)),
            pltpu.SemaphoreType.DMA((row_blocks - 1,)),
            pltpu.SemaphoreType.DMA((row_blocks - 1,)),
            pltpu.SemaphoreType.DMA((col_blocks - 1,)),
            pltpu.SemaphoreType.DMA((col_blocks - 1,)),
            pltpu.SemaphoreType.DMA((chunks, col_blocks - 1)),
            pltpu.SemaphoreType.DMA((chunks, col_blocks - 1)),
            pltpu.SemaphoreType.DMA((chunks, row_blocks)),
            pltpu.SemaphoreType.DMA((chunks, row_blocks)),
            pltpu.SemaphoreType.DMA((chunks, row_blocks)),
            pltpu.SemaphoreType.DMA((parts, doms - 1, 2)),
            pltpu.SemaphoreType.DMA((parts, doms - 1, 2)),
            pltpu.SemaphoreType.DMA((parts, doms - 1)),
            pltpu.SemaphoreType.DMA((parts, doms - 1)),
        ],
        compiler_params=pltpu.CompilerParams(
            collective_id=0, has_side_effects=True, vmem_limit_bytes=44 << 20
        ),
    )(feats, cots, weights[0, 0])
    return merged[None]


def solution(mesh):
    return jax.shard_map(
        body,
        mesh=mesh,
        in_specs=(
            P("dom", "fsdp", None, None),
            P("dom", None, "fsdp", None),
            P("dom", None, "fsdp", None),
            P("dom", None, "fsdp"),
        ),
        out_specs=P("fsdp", None, None),
        check_vma=False,
    )
```
